256 devices in a mesh: dp: 4 (over y), ctx: 8 (over z), head: 8 (over x, core).
Axes of the slice: x: 4, y: 4, z: 8, core: 2. Of those that a mesh axis runs over, the one named last changes fastest.
Arguments:
- query: bfloat16 [4, 1024, 12288], P('dp', 'ctx', 'head'), may hold values from -180 to 180
- latent: bfloat16 [4, 1024, 576], P('dp', ('ctx', 'head')), may hold values from -6 to 6
- w_uk: bfloat16 [512, 8192], P(None, 'head'), may hold values from -0.25 to 0.25
- w_uv: bfloat16 [512, 8192], P(None, 'head'), may hold values from -0.25 to 0.25
- grad_out: bfloat16 [4, 1024, 8192], P('dp', 'ctx', 'head'), may hold values from -6 to 6
- block_order: int32 [16], replicated, may hold values from 0 to 15, as said below
Outputs:
- grad_query: bfloat16 [4, 1024, 12288], P('dp', 'ctx', 'head')
- grad_latent: float32 [4, 1024, 576], P('dp', ('ctx', 'head'))
- grad_w_uk: float32 [512, 8192], P(None, 'head')
- grad_w_uv: float32 [512, 8192], P(None, 'head')
The draws below stay inside these ranges and needn't reach their ends.
Inputs may be any that keep to these rules, and one draw needn't show every extreme that they name: `block_order`: a permutation of the blocks in which storage blocks 2 r and 2 r + 1 hold blocks whose numbers add up to 15.
All inputs are finite; a program needn't handle non-finite values.
Results may differ from the reference program's by a relative error of at most 0.015.
Values may be sent and summed in bfloat16 or wider, within the bound.
No kernel may reach another device: no remote copies, remote signals or barrier semaphores. Data moves between devices by JAX's collectives and lax.ppermute only.
A program may use at most 64 MiB of HBM per device.

```python
import jax
import jax.numpy as jnp
from jax import lax

LAT = 512
ROPE = 64
NOPE = 128
VDIM = 128
HEADS = 64
TOK_DEV = 128
SEQ = 1024
BLOCKS = 16
SEQS = 4


def draw_both(key):
    base = jax.random.fold_in(key, 41)
    key_lat, key_query = jax.random.split(base, 2)
    width = NOPE + ROPE
    latent = jnp.clip(jax.random.normal(key_lat, (SEQS, SEQ, LAT + ROPE), jnp.float32), -6.0, 6.0)
    query = jnp.clip(jax.random.normal(key_query, (SEQS, SEQ, HEADS, width), jnp.float32), -6.0, 6.0)
    return (latent, query.reshape(SEQS, SEQ, HEADS * width))


def draw_query(key, part):
    latent, query = draw_both(key)
    return query.astype(jnp.bfloat16)


def draw_latent(key, part):
    latent, query = draw_both(key)
    return latent.astype(jnp.bfloat16)


def draw_block_order(key, part):
    key_perm, key_flip = jax.random.split(jax.random.fold_in(key, 11))
    count = BLOCKS // 2
    lower = jax.random.permutation(key_perm, count).astype(jnp.int32)
    flip = jax.random.randint(key_flip, (count,), 0, 2)
    first = jnp.where(flip == 1, BLOCKS - 1 - lower, lower)
    second = BLOCKS - 1 - first
    return jnp.stack([first, second], axis=1).reshape(BLOCKS).astype(jnp.int32)


def block_levels(own_key, extent, cuts, smallest, high):
    def one(dim, parts):
        draws = jax.random.uniform(jax.random.fold_in(jax.random.fold_in(own_key, 6), dim), (parts,), jnp.float32, smallest / len(cuts), high / len(cuts))
        return jnp.repeat(jnp.exp(draws), extent[dim] // parts).reshape((-1,) + (1,) * (len(extent) - dim - 1))

    loudness = one(*cuts[0])
    for cut in cuts[1:]:
        loudness = loudness * one(*cut)
    return loudness


def gaussian(own_key, shape, scale, limit, shards=(), held_as=jnp.bfloat16):
    level = block_levels(own_key, shape, shards, -0.22, 0.18) if shards else 1.0
    array = jax.random.normal(own_key, shape, jnp.float32) * scale * level
    return jnp.minimum(jnp.maximum(array, -limit), limit).astype(held_as)


def setup_inputs(seed: int = 0) -> dict:
    seeds = jax.random.split(jax.random.key(seed), 7)
    query = draw_query(jax.random.fold_in(seeds[6], 71), 0)
    latent = draw_latent(jax.random.fold_in(seeds[6], 71), 0)
    w_uk = gaussian(seeds[2], (LAT, HEADS * NOPE), LAT ** -0.5, 0.25, ((1, 8),))
    w_uv = gaussian(seeds[3], (LAT, HEADS * VDIM), LAT ** -0.5, 0.25, ((1, 8),))
    grad_out = gaussian(seeds[4], (SEQS, SEQ, HEADS * VDIM), 1.0, 6.0, ((0, 4), (1, 8), (2, 8)))
    block_order = draw_block_order(jax.random.fold_in(seeds[6], 71), 0)
    return dict(query=query, latent=latent, w_uk=w_uk, w_uv=w_uv, grad_out=grad_out, block_order=block_order)


def reference(query, latent, w_uk, w_uv, grad_out, block_order):
    width = NOPE + ROPE
    scale = width ** -0.5
    half = TOK_DEV // 2
    seq = query.shape[1]
    index = jnp.arange(seq, dtype=jnp.int32)
    positions = block_order[index // half] * half + index % half
    allowed = positions[None, :] <= positions[:, None]
    w_uk_wide = w_uk.astype(jnp.float32)
    w_uv_wide = w_uv.astype(jnp.float32)
    high = lax.Precision.HIGHEST
    grads_query = []
    grads_latent = []
    grad_w_uk = jnp.zeros(w_uk.shape, jnp.float32)
    grad_w_uv = jnp.zeros(w_uv.shape, jnp.float32)
    for replica in range(SEQS):
        latent_c = latent[replica, :, :LAT]
        rope = latent[replica, :, LAT:]
        keys = jnp.dot(latent_c, w_uk, preferred_element_type=jnp.float32).astype(jnp.bfloat16)
        values = jnp.dot(latent_c, w_uv, preferred_element_type=jnp.float32).astype(jnp.bfloat16)
        q_rows = query[replica]
        d_rows = grad_out[replica]

        def one_head(head_id):
            q_head = lax.dynamic_slice_in_dim(q_rows, head_id * width, width, 1)
            k_head = jnp.concatenate([lax.dynamic_slice_in_dim(keys, head_id * NOPE, NOPE, 1), rope], axis=1)
            v_head = lax.dynamic_slice_in_dim(values, head_id * VDIM, VDIM, 1)
            d_head = lax.dynamic_slice_in_dim(d_rows, head_id * VDIM, VDIM, 1)
            scores = jnp.dot(q_head, k_head.T, preferred_element_type=jnp.float32) * scale
            masked = jnp.where(allowed, scores, -jnp.inf)
            top = jnp.max(masked, axis=1, keepdims=True)
            weights = jnp.where(allowed, jnp.exp(masked - top), 0.0)
            probs = weights / jnp.sum(weights, axis=1, keepdims=True)
            probs_b = probs.astype(jnp.bfloat16)
            out = jnp.dot(probs_b, v_head, preferred_element_type=jnp.float32)
            drow = jnp.sum(d_head.astype(jnp.float32) * out, axis=1, keepdims=True)
            dprob = jnp.dot(d_head, v_head.T, preferred_element_type=jnp.float32)
            dscore = (probs * (dprob - drow)).astype(jnp.bfloat16)
            grad_q = jnp.dot(dscore, k_head, preferred_element_type=jnp.float32) * scale
            grad_k = jnp.dot(dscore.T, q_head, preferred_element_type=jnp.float32) * scale
            grad_v = jnp.dot(probs_b.T, d_head, preferred_element_type=jnp.float32)
            return grad_q, grad_k, grad_v

        grad_q, grad_k, grad_v = lax.map(one_head, jnp.arange(HEADS, dtype=jnp.int32))
        grads_query.append(grad_q.transpose(1, 0, 2).reshape(seq, HEADS * width).astype(jnp.bfloat16))
        dkey_nope = grad_k[:, :, :NOPE].transpose(1, 0, 2).reshape(seq, HEADS * NOPE)
        drope = jnp.sum(grad_k[:, :, NOPE:], axis=0)
        dvalue = grad_v.transpose(1, 0, 2).reshape(seq, HEADS * VDIM)
        grad_c = jnp.dot(dkey_nope, w_uk_wide.T, precision=high) + jnp.dot(dvalue, w_uv_wide.T, precision=high)
        grads_latent.append(jnp.concatenate([grad_c, drope], axis=1))
        latent_wide = latent_c.astype(jnp.float32)
        grad_w_uk = grad_w_uk + jnp.dot(latent_wide.T, dkey_nope, precision=high)
        grad_w_uv = grad_w_uv + jnp.dot(latent_wide.T, dvalue, precision=high)
    return jnp.stack(grads_query), jnp.stack(grads_latent), grad_w_uk, grad_w_uv
```

```python
import functools

import jax
import jax.numpy as jnp
from jax import lax
from jax.experimental import pallas as pl
from jax.experimental.pallas import tpu as pltpu
from jax.sharding import PartitionSpec as P

LAT = 512
ROPE = 64
NOPE = 128
VDIM = 128
WIDTH = NOPE + ROPE
HALF = 64
SUB = 16
TILE = 256
BF = jnp.bfloat16
F32 = jnp.float32
VMEM = pl.BlockSpec(memory_space=pltpu.VMEM)

ROW_DO = NOPE
ROW_ROPE = ROW_DO + VDIM
ROW_LAT = ROW_ROPE + ROPE
ROW_LROPE = ROW_LAT + SUB * (LAT // 128)
ROWS_IN = ROW_LROPE + SUB
ROW_GROPE = NOPE
ROW_GL = ROW_GROPE + ROPE
ROW_GLROPE = ROW_GL + SUB * (LAT // 128)
ROWS_OUT = ROW_GLROPE + SUB


def dot_nn(a, b):
    return lax.dot_general(a, b, (((1,), (0,)), ((), ())), preferred_element_type=F32)


def dot_nt(a, b):
    return lax.dot_general(a, b, (((1,), (1,)), ((), ())), preferred_element_type=F32)


def dot_tn(a, b):
    return lax.dot_general(a, b, (((0,), (0,)), ((), ())), preferred_element_type=F32)


def pack_kernel(q_ref, d_ref, lat_ref, out_ref):
    n = out_ref.shape[0]
    for h in range(n):
        q = q_ref[:, h * WIDTH : (h + 1) * WIDTH]
        out_ref[h, 0:ROW_DO, :] = q[:, :NOPE]
        out_ref[h, ROW_DO:ROW_ROPE, :] = d_ref[:, h * VDIM : (h + 1) * VDIM]
        rope = q[:, NOPE:]
        out_ref[h, ROW_ROPE:ROW_LAT, :] = jnp.concatenate([rope[:HALF], rope[HALF:]], axis=1)
        for j in range(LAT // 128):
            out_ref[h, ROW_LAT + SUB * j : ROW_LAT + SUB * (j + 1), :] = lat_ref[
                :, 128 * j : 128 * (j + 1)
            ]
        rope_k = lat_ref[:, LAT:]
        out_ref[h, ROW_LROPE:ROWS_IN, :] = jnp.concatenate([rope_k, rope_k], axis=1)


def attention_kernel(
    order_ref, rank_ref, in_ref, lat_in_ref, wk_ref, wv_ref,
    gl_ref, gq_ref, gw_ref,
    lat_s, k_s, v_s, q_s, d_s, dk_s, dv_s, dq_s, gl_s,
):
    blocks = in_ref.shape[0]
    parts = lat_in_ref.shape[0]
    seq = lat_s.shape[0]
    scale = WIDTH ** (-0.5)
    per_half = HALF // SUB

    def place(block):
        return pl.multiple_of(order_ref[block] * HALF, HALF)

    for s in range(blocks):
        for half in range(2):
            base = place(2 * s + half)
            rows = pl.ds(base, HALF)
            lo = half * HALF
            q_s[rows, :NOPE] = in_ref[s, lo : lo + HALF, :]
            q_s[rows, NOPE:] = in_ref[s, ROW_ROPE:ROW_LAT, half * ROPE : (half + 1) * ROPE]
            d_s[rows, :] = in_ref[s, ROW_DO + lo : ROW_DO + lo + HALF, :]
            for i in range(per_half):
                p = half * per_half + i
                sub = pl.ds(pl.multiple_of(base + i * SUB, SUB), SUB)
                for j in range(LAT // 128):
                    lat_s[sub, 128 * j : 128 * (j + 1)] = lat_in_ref[p, s, SUB * j : SUB * (j + 1), :]
                k_s[sub, NOPE:] = lat_in_ref[p, s, SUB * (LAT // 128) :, :ROPE]

    w_both = jnp.concatenate([wk_ref[...], wv_ref[...]], axis=1)
    for t in range(seq // TILE):
        rows = slice(t * TILE, (t + 1) * TILE)
        both = dot_nn(lat_s[rows, :], w_both)
        k_s[rows, :NOPE] = both[:, :NOPE].astype(BF)
        v_s[rows, :] = both[:, NOPE:].astype(BF)

    dk_s[...] = jnp.zeros_like(dk_s)
    dv_s[...] = jnp.zeros_like(dv_s)
    for t in range(seq // TILE):
        rows = slice(t * TILE, (t + 1) * TILE)
        width = (t + 1) * TILE
        q = q_s[rows, :]
        d = d_s[rows, :]
        k = k_s[:width, :]
        scores = dot_nt(k, q) * scale
        key_pos = lax.broadcasted_iota(jnp.int32, (width, TILE), 0)
        row_pos = lax.broadcasted_iota(jnp.int32, (width, TILE), 1) + t * TILE
        masked = jnp.where(key_pos <= row_pos, scores, -jnp.inf)
        top = jnp.max(masked, axis=0, keepdims=True)
        weights = jnp.exp(masked - top)
        probs = weights / jnp.sum(weights, axis=0, keepdims=True)
        probs_b = probs.astype(BF)
        dprob = dot_nt(v_s[:width, :], d)
        drow = jnp.sum(probs_b.astype(F32) * dprob, axis=0, keepdims=True)
        dscore = (probs * (dprob - drow)).astype(BF)
        dq_s[rows, :] = (dot_tn(dscore, k) * scale).astype(BF)
        dk_s[:width, :] += dot_nn(dscore, q)
        dv_s[:width, :] += dot_nn(probs_b, d)

    dk = dk_s[...] * scale
    dkv = jnp.concatenate([dk[:, :NOPE], dv_s[...]], axis=1).astype(BF)
    gw = dot_tn(lat_s[...], dkv).astype(BF)
    n = gw_ref.shape[0]
    share = LAT // n
    for i in range(n):
        gw_ref[i] = gw[i * share : (i + 1) * share]
    gl_s[:, :LAT] = dot_nt(dkv, w_both).astype(BF)
    gl_s[:, LAT:] = dk[:, NOPE:].astype(BF)

    for s in range(blocks):
        for half in range(2):
            base = place(2 * s + half)
            rows = pl.ds(base, HALF)
            lo = half * HALF
            gq_ref[s, lo : lo + HALF, :] = dq_s[rows, :NOPE]
            gq_ref[s, ROW_GROPE:ROW_GL, half * ROPE : (half + 1) * ROPE] = dq_s[rows, NOPE:]
            for i in range(per_half):
                p = half * per_half + i
                sub = pl.ds(pl.multiple_of(base + i * SUB, SUB), SUB)
                for j in range(LAT // 128):
                    gl_ref[p, s, SUB * j : SUB * (j + 1), :] = gl_s[sub, 128 * j : 128 * (j + 1)]
                rope = gl_s[sub, LAT:]
                gl_ref[p, s, SUB * (LAT // 128) :, :] = jnp.concatenate([rope, rope], axis=1)


def unpack_kernel(in_ref, gq_ref, gl_ref):
    n = in_ref.shape[0]
    for h in range(n):
        rope = in_ref[h, ROW_GROPE:ROW_GL, :]
        rope = jnp.concatenate([rope[:, :ROPE], rope[:, ROPE:]], axis=0)
        gq_ref[:, h * WIDTH : (h + 1) * WIDTH] = jnp.concatenate([in_ref[h, :NOPE, :], rope], axis=1)
    for j in range(LAT // 128):
        part = in_ref[:, ROW_GL + SUB * j : ROW_GL + SUB * (j + 1), :].astype(F32)
        gl_ref[:, 128 * j : 128 * (j + 1)] = jnp.sum(part, axis=0)
    part = in_ref[:, ROW_GLROPE:ROWS_OUT, :ROPE].astype(F32)
    gl_ref[:, LAT:] = jnp.sum(part, axis=0)


def on_device(n_dp, n_ctx, n_head, query, latent, w_uk, w_uv, grad_out, block_order):
    seq = n_ctx * n_head * SUB
    rows = query.shape[1]
    rank = lax.axis_index("ctx").astype(jnp.int32).reshape(1)
    packed = pl.pallas_call(
        pack_kernel,
        out_shape=jax.ShapeDtypeStruct((n_ctx, ROWS_IN, 128), BF),
        in_specs=[VMEM] * 3,
        out_specs=VMEM,
        name="pack",
    )(query[0], grad_out[0], latent[0])
    mine = lax.all_to_all(packed, "ctx", 0, 0, tiled=True)
    lat_mine = mine[:, ROW_LAT:ROWS_IN, :]
    lat_rows = lat_mine.shape[1]
    lat_all = lax.all_to_all(
        jnp.broadcast_to(lat_mine[None], (n_head,) + lat_mine.shape), "head", 0, 0, tiled=True
    )
    full = lambda shape: pl.BlockSpec(shape, lambda i, order, rank: (0,) * len(shape))
    head_cols = pl.BlockSpec((LAT, NOPE), lambda i, order, rank: (0, rank[0]))
    gl_part, gq_part, gw_part = pl.pallas_call(
        attention_kernel,
        grid_spec=pltpu.PrefetchScalarGridSpec(
            num_scalar_prefetch=2,
            grid=(1,),
            in_specs=[full(mine.shape), full(lat_all.shape), head_cols, head_cols],
            out_specs=[
                full((n_head, n_ctx, lat_rows, 128)),
                full((n_ctx, ROW_GL, 128)),
                full((n_dp, LAT // n_dp, NOPE + VDIM)),
            ],
            scratch_shapes=[
                pltpu.VMEM((seq, LAT), BF),
                pltpu.VMEM((seq, WIDTH), BF),
                pltpu.VMEM((seq, VDIM), BF),
                pltpu.VMEM((seq, WIDTH), BF),
                pltpu.VMEM((seq, VDIM), BF),
                pltpu.VMEM((seq, WIDTH), F32),
                pltpu.VMEM((seq, VDIM), F32),
                pltpu.VMEM((seq, WIDTH), BF),
                pltpu.VMEM((seq, LAT + ROPE), BF),
            ],
        ),
        out_shape=[
            jax.ShapeDtypeStruct((n_head, n_ctx, lat_rows, 128), BF),
            jax.ShapeDtypeStruct((n_ctx, ROW_GL, 128), BF),
            jax.ShapeDtypeStruct((n_dp, LAT // n_dp, NOPE + VDIM), BF),
        ],
        compiler_params=pltpu.CompilerParams(vmem_limit_bytes=48 * 1024 * 1024),
        cost_estimate=pl.CostEstimate(
            flops=3 * 10**9, bytes_accessed=5 * 10**6, transcendentals=seq * seq
        ),
        name="attention_backward",
    )(block_order, rank, mine, lat_all, w_uk, w_uv)

    gw_sum = jnp.sum(lax.all_to_all(gw_part, "dp", 0, 0, tiled=True).astype(F32), axis=0).astype(BF)
    gw_ctx = lax.all_to_all(
        jnp.broadcast_to(gw_sum[None], (n_ctx,) + gw_sum.shape), "ctx", 0, 0, tiled=True
    )
    gw_all = lax.all_to_all(
        jnp.broadcast_to(gw_ctx[None], (n_dp,) + gw_ctx.shape), "dp", 0, 0, tiled=True
    )
    gw_all = gw_all.transpose(0, 2, 1, 3).reshape(LAT, n_ctx, NOPE + VDIM).astype(F32)
    grad_w_uk = gw_all[:, :, :NOPE].reshape(LAT, n_ctx * NOPE)
    grad_w_uv = gw_all[:, :, NOPE:].reshape(LAT, n_ctx * VDIM)

    gl_head = jnp.sum(
        lax.all_to_all(gl_part, "head", 0, 0, tiled=True).astype(F32), axis=0
    ).astype(BF)
    back = lax.all_to_all(jnp.concatenate([gq_part, gl_head], axis=1), "ctx", 0, 0, tiled=True)
    grad_query, grad_latent = pl.pallas_call(
        unpack_kernel,
        out_shape=[
            jax.ShapeDtypeStruct((rows, n_ctx * WIDTH), BF),
            jax.ShapeDtypeStruct((SUB, LAT + ROPE), F32),
        ],
        in_specs=[VMEM],
        out_specs=[VMEM, VMEM],
        name="unpack",
    )(back)
    return (grad_query[None], grad_latent[None], grad_w_uk, grad_w_uv)


def solution(mesh):
    sizes = mesh.shape
    return jax.shard_map(
        functools.partial(on_device, sizes["dp"], sizes["ctx"], sizes["head"]),
        mesh=mesh,
        in_specs=(
            P("dp", "ctx", "head"),
            P("dp", ("ctx", "head"), None),
            P(None, "head"),
            P(None, "head"),
            P("dp", "ctx", "head"),
            P(),
        ),
        out_specs=(
            P("dp", "ctx", "head"),
            P("dp", ("ctx", "head"), None),
            P(None, "head"),
            P(None, "head"),
        ),
        check_vma=False,
    )
```

```python
import functools

import jax
import jax.numpy as jnp
from jax import lax
from jax.experimental import pallas as pl
from jax.experimental.pallas import tpu as pltpu
from jax.sharding import PartitionSpec as P

LAT = 512
ROPE = 64
NOPE = 128
VDIM = 128
WIDTH = NOPE + ROPE
HALF = 64
SUB = 16
TILE = 256
BF = jnp.bfloat16
F32 = jnp.float32
VMEM = pl.BlockSpec(memory_space=pltpu.VMEM)

ROW_DO = NOPE
ROW_ROPE = ROW_DO + VDIM
ROWS_IN = ROW_ROPE + ROPE
ROW_GROPE = NOPE
ROW_GL = ROW_GROPE + ROPE
ROW_GLROPE = ROW_GL + SUB * (LAT // 128)
ROWS_OUT = ROW_GLROPE + SUB


def dot_nn(a, b):
    return lax.dot_general(a, b, (((1,), (0,)), ((), ())), preferred_element_type=F32)


def dot_nt(a, b):
    return lax.dot_general(a, b, (((1,), (1,)), ((), ())), preferred_element_type=F32)


def dot_tn(a, b):
    return lax.dot_general(a, b, (((0,), (0,)), ((), ())), preferred_element_type=F32)


def pack_kernel(rank_ref, q_ref, d_ref, wk_ref, wv_ref, out_ref, w_ref):
    n = out_ref.shape[0]
    for h in range(n):
        q = q_ref[:, h * WIDTH : (h + 1) * WIDTH]
        out_ref[h, 0:ROW_DO, :] = q[:, :NOPE]
        out_ref[h, ROW_DO:ROW_ROPE, :] = d_ref[:, h * VDIM : (h + 1) * VDIM]
        rope = q[:, NOPE:]
        out_ref[h, ROW_ROPE:ROWS_IN, :] = jnp.concatenate([rope[:HALF], rope[HALF:]], axis=1)
    w_ref[:, :NOPE] = wk_ref[...]
    w_ref[:, NOPE:] = wv_ref[...]


def attention_kernel(n_head, n_dp, order_ref, rank_ref, in_ref, w_ref, *refs):
    lat_refs, refs = refs[:n_head], refs[n_head:]
    gl_ref, gq_ref = refs[:2]
    gw_refs = refs[2 : 2 + n_dp]
    lat_s, k_s, v_s, q_s, d_s, dk_s, dv_s, dq_s, gl_s, gw_s = refs[2 + n_dp :]
    blocks = in_ref.shape[0]
    seq = lat_s.shape[0]
    scale = WIDTH ** (-0.5)
    per_half = HALF // SUB

    def place(block):
        return pl.multiple_of(order_ref[block] * HALF, HALF)

    for s in range(blocks):
        for half in range(2):
            rows = pl.ds(place(2 * s + half), HALF)
            lo = half * HALF
            q_s[rows, :NOPE] = in_ref[s, lo : lo + HALF, :]
            q_s[rows, NOPE:] = in_ref[s, ROW_ROPE:ROWS_IN, half * ROPE : (half + 1) * ROPE]
            d_s[rows, :] = in_ref[s, ROW_DO + lo : ROW_DO + lo + HALF, :]
    for shift in range(n_head):
        p = lax.rem(rank_ref[1] + n_head - shift, n_head)
        half, i = lax.div(p, per_half), lax.rem(p, per_half)
        for s in range(blocks):
            sub = pl.ds(pl.multiple_of(order_ref[2 * s + half] * HALF + i * SUB, SUB), SUB)
            lat_s[sub, :] = lat_refs[shift][s, :, :LAT]
            k_s[sub, NOPE:] = lat_refs[shift][s, :, LAT:]

    w_both = w_ref[...]
    for t in range(seq // TILE):
        rows = slice(t * TILE, (t + 1) * TILE)
        both = dot_nn(lat_s[rows, :], w_both)
        k_s[rows, :NOPE] = both[:, :NOPE].astype(BF)
        v_s[rows, :] = both[:, NOPE:].astype(BF)

    dk_s[...] = jnp.zeros_like(dk_s)
    dv_s[...] = jnp.zeros_like(dv_s)
    for t in range(seq // TILE):
        rows = slice(t * TILE, (t + 1) * TILE)
        width = (t + 1) * TILE
        q = q_s[rows, :]
        d = d_s[rows, :]
        k = k_s[:width, :]
        scores = dot_nt(k, q) * scale
        key_pos = lax.broadcasted_iota(jnp.int32, (width, TILE), 0)
        row_pos = lax.broadcasted_iota(jnp.int32, (width, TILE), 1) + t * TILE
        masked = jnp.where(key_pos <= row_pos, scores, -jnp.inf)
        top = jnp.max(masked, axis=0, keepdims=True)
        weights = jnp.exp(masked - top)
        probs = weights / jnp.sum(weights, axis=0, keepdims=True)
        probs_b = probs.astype(BF)
        dprob = dot_nt(v_s[:width, :], d)
        drow = jnp.sum(probs_b.astype(F32) * dprob, axis=0, keepdims=True)
        dscore = (probs * (dprob - drow)).astype(BF)
        dq_s[rows, :] = (dot_tn(dscore, k) * scale).astype(BF)
        dk_s[:width, :] += dot_nn(dscore, q)
        dv_s[:width, :] += dot_nn(probs_b, d)

    dk = dk_s[...] * scale
    dkv = jnp.concatenate([dk[:, :NOPE], dv_s[...]], axis=1).astype(BF)
    gw_s[...] = dot_tn(lat_s[...], dkv).astype(BF)
    share = LAT // n_dp
    for shift in range(n_dp):
        target = lax.rem(rank_ref[2] + shift, n_dp)
        gw_refs[shift][...] = gw_s[pl.ds(pl.multiple_of(target * share, share), share), :]
    gl_s[:, :LAT] = dot_nt(dkv, w_both).astype(BF)
    gl_s[:, LAT:] = dk[:, NOPE:].astype(BF)

    for s in range(blocks):
        for half in range(2):
            base = place(2 * s + half)
            rows = pl.ds(base, HALF)
            lo = half * HALF
            gq_ref[s, lo : lo + HALF, :] = dq_s[rows, :NOPE]
            gq_ref[s, ROW_GROPE:ROW_GL, half * ROPE : (half + 1) * ROPE] = dq_s[rows, NOPE:]
            for i in range(per_half):
                p = half * per_half + i
                sub = pl.ds(pl.multiple_of(base + i * SUB, SUB), SUB)
                for j in range(LAT // 128):
                    gl_ref[p, s, SUB * j : SUB * (j + 1), :] = gl_s[sub, 128 * j : 128 * (j + 1)]
                rope = gl_s[sub, LAT:]
                gl_ref[p, s, SUB * (LAT // 128) :, :] = jnp.concatenate([rope, rope], axis=1)


def unpack_kernel(in_ref, gq_ref, gl_ref):
    n = in_ref.shape[0]
    for h in range(n):
        rope = in_ref[h, ROW_GROPE:ROW_GL, :]
        rope = jnp.concatenate([rope[:, :ROPE], rope[:, ROPE:]], axis=0)
        gq_ref[:, h * WIDTH : (h + 1) * WIDTH] = jnp.concatenate([in_ref[h, :NOPE, :], rope], axis=1)
    for j in range(LAT // 128):
        part = in_ref[:, ROW_GL + SUB * j : ROW_GL + SUB * (j + 1), :].astype(F32)
        gl_ref[:, 128 * j : 128 * (j + 1)] = jnp.sum(part, axis=0)
    part = in_ref[:, ROW_GLROPE:ROWS_OUT, :ROPE].astype(F32)
    gl_ref[:, LAT:] = jnp.sum(part, axis=0)


def assemble_kernel(n_dp, rank_ref, *refs):
    part_refs, (gk_ref, gv_ref) = refs[:n_dp], refs[n_dp:]
    n_ctx, share, _ = part_refs[0].shape
    for shift in range(n_dp):
        source = lax.rem(rank_ref[2] + n_dp - shift, n_dp)
        rows = pl.ds(pl.multiple_of(source * share, share), share)
        for h in range(n_ctx):
            part = part_refs[shift][h].astype(F32)
            gk_ref[rows, h * NOPE : (h + 1) * NOPE] = part[:, :NOPE]
            gv_ref[rows, h * VDIM : (h + 1) * VDIM] = part[:, NOPE:]


def shifted(x, axis, n, shift):
    return lax.ppermute(x, axis, [(i, (i + shift) % n) for i in range(n)])


def whole(shape):
    return pl.BlockSpec(shape, lambda i, *scalars: (0,) * len(shape))


def call(kernel, name, scalars, inputs, outs, scratch=(), in_specs=None, flops=0):
    moved = sum(x.size * x.dtype.itemsize for x in inputs) + sum(
        x.size * x.dtype.itemsize for x in outs
    )
    return pl.pallas_call(
        kernel,
        grid_spec=pltpu.PrefetchScalarGridSpec(
            num_scalar_prefetch=len(scalars),
            grid=(1,),
            in_specs=in_specs or [whole(x.shape) for x in inputs],
            out_specs=[whole(x.shape) for x in outs],
            scratch_shapes=list(scratch),
        ),
        out_shape=list(outs),
        compiler_params=pltpu.CompilerParams(vmem_limit_bytes=48 * 1024 * 1024),
        cost_estimate=pl.CostEstimate(flops=flops, bytes_accessed=moved, transcendentals=0),
        name=name,
    )(*scalars, *inputs)


def on_device(n_dp, n_ctx, n_head, query, latent, w_uk, w_uv, grad_out, block_order):
    seq = n_ctx * n_head * SUB
    rows = query.shape[1]
    shape = jax.ShapeDtypeStruct
    ranks = jnp.stack([lax.axis_index(a).astype(jnp.int32) for a in ("ctx", "head", "dp")])

    lat_mine = lax.all_to_all(
        jnp.broadcast_to(latent, (n_ctx, SUB, LAT + ROPE)), "ctx", 0, 0, tiled=True
    )
    lat_all = [lat_mine] + [shifted(lat_mine, "head", n_head, i) for i in range(1, n_head)]
    head_cols = pl.BlockSpec((LAT, NOPE), lambda i, rank: (0, rank[0]))
    packed, w_both = call(
        pack_kernel,
        "pack",
        (ranks,),
        (query[0], grad_out[0], w_uk, w_uv),
        [shape((n_ctx, ROWS_IN, 128), BF), shape((LAT, NOPE + VDIM), BF)],
        in_specs=[whole(query.shape[1:]), whole(grad_out.shape[1:]), head_cols, head_cols],
    )
    mine = lax.all_to_all(packed, "ctx", 0, 0, tiled=True)

    gl_part, gq_part, *gw_parts = call(
        functools.partial(attention_kernel, n_head, n_dp),
        "attention_backward",
        (block_order, ranks),
        (mine, w_both, *lat_all),
        [
            shape((n_head, n_ctx, SUB * (LAT // 128) + SUB, 128), BF),
            shape((n_ctx, ROW_GL, 128), BF),
        ]
        + [shape((LAT // n_dp, NOPE + VDIM), BF)] * n_dp,
        scratch=[
            pltpu.VMEM((seq, LAT), BF),
            pltpu.VMEM((seq, WIDTH), BF),
            pltpu.VMEM((seq, VDIM), BF),
            pltpu.VMEM((seq, WIDTH), BF),
            pltpu.VMEM((seq, VDIM), BF),
            pltpu.VMEM((seq, WIDTH), F32),
            pltpu.VMEM((seq, VDIM), F32),
            pltpu.VMEM((seq, WIDTH), BF),
            pltpu.VMEM((seq, LAT + ROPE), BF),
            pltpu.VMEM((LAT, NOPE + VDIM), BF),
        ],
        flops=3 * 10**9,
    )

    gw_sum = gw_parts[0].astype(F32)
    for i in range(1, n_dp):
        gw_sum = gw_sum + shifted(gw_parts[i], "dp", n_dp, i).astype(F32)
    gw_sum = gw_sum.astype(BF)
    gw_ctx = lax.all_to_all(
        jnp.broadcast_to(gw_sum[None], (n_ctx,) + gw_sum.shape), "ctx", 0, 0, tiled=True
    )
    gw_all = [gw_ctx] + [shifted(gw_ctx, "dp", n_dp, i) for i in range(1, n_dp)]
    grad_w_uk, grad_w_uv = call(
        functools.partial(assemble_kernel, n_dp),
        "assemble",
        (ranks,),
        gw_all,
        [shape((LAT, n_ctx * NOPE), F32), shape((LAT, n_ctx * VDIM), F32)],
    )

    gl_head = jnp.sum(
        lax.all_to_all(gl_part, "head", 0, 0, tiled=True).astype(F32), axis=0
    ).astype(BF)
    back = lax.all_to_all(jnp.concatenate([gq_part, gl_head], axis=1), "ctx", 0, 0, tiled=True)
    grad_query, grad_latent = pl.pallas_call(
        unpack_kernel,
        out_shape=[
            jax.ShapeDtypeStruct((rows, n_ctx * WIDTH), BF),
            jax.ShapeDtypeStruct((SUB, LAT + ROPE), F32),
        ],
        in_specs=[VMEM],
        out_specs=[VMEM, VMEM],
        name="unpack",
    )(back)
    return (grad_query[None], grad_latent[None], grad_w_uk, grad_w_uv)


def solution(mesh):
    sizes = mesh.shape
    return jax.shard_map(
        functools.partial(on_device, sizes["dp"], sizes["ctx"], sizes["head"]),
        mesh=mesh,
        in_specs=(
            P("dp", "ctx", "head"),
            P("dp", ("ctx", "head"), None),
            P(None, "head"),
            P(None, "head"),
            P("dp", "ctx", "head"),
            P(),
        ),
        out_specs=(
            P("dp", "ctx", "head"),
            P("dp", ("ctx", "head"), None),
            P(None, "head"),
            P(None, "head"),
        ),
        check_vma=False,
    )
```

```python
import functools

import jax
import jax.numpy as jnp
from jax import lax
from jax.experimental import pallas as pl
from jax.experimental.pallas import tpu as pltpu
from jax.sharding import PartitionSpec as P

LAT = 512
ROPE = 64
NOPE = 128
VDIM = 128
WIDTH = NOPE + ROPE
HALF = 64
SUB = 16
TILE = 256
BF = jnp.bfloat16
F32 = jnp.float32
VMEM = pl.BlockSpec(memory_space=pltpu.VMEM)

ROW_DO = NOPE
ROW_ROPE = ROW_DO + VDIM
ROWS_IN = ROW_ROPE + ROPE
ROW_GROPE = NOPE
ROW_GL = ROW_GROPE + ROPE
ROW_GLROPE = ROW_GL + SUB * (LAT // 128)
ROWS_OUT = ROW_GLROPE + SUB


def dot_nn(a, b):
    return lax.dot_general(a, b, (((1,), (0,)), ((), ())), preferred_element_type=F32)


def dot_nt(a, b):
    return lax.dot_general(a, b, (((1,), (1,)), ((), ())), preferred_element_type=F32)


def dot_tn(a, b):
    return lax.dot_general(a, b, (((0,), (0,)), ((), ())), preferred_element_type=F32)


def pack_kernel(rank_ref, q_ref, d_ref, wk_ref, wv_ref, out_ref, w_ref):
    n = out_ref.shape[0]
    for h in range(n):
        q = q_ref[:, h * WIDTH : (h + 1) * WIDTH]
        out_ref[h, 0:ROW_DO, :] = q[:, :NOPE]
        out_ref[h, ROW_DO:ROW_ROPE, :] = d_ref[:, h * VDIM : (h + 1) * VDIM]
        rope = q[:, NOPE:]
        out_ref[h, ROW_ROPE:ROWS_IN, :] = jnp.concatenate([rope[:HALF], rope[HALF:]], axis=1)
    w_ref[:, :NOPE] = wk_ref[...]
    w_ref[:, NOPE:] = wv_ref[...]


def attention_kernel(n_head, n_dp, order_ref, rank_ref, in_ref, w_ref, *refs):
    lat_refs, refs = refs[:n_head], refs[n_head:]
    gl_ref, gq_ref = refs[:2]
    gw_refs = refs[2 : 2 + n_dp]
    lat_s, k_s, v_s, q_s, d_s, dk_s, dv_s, dq_s, gl_s, gw_s = refs[2 + n_dp :]
    blocks = in_ref.shape[0]
    seq = lat_s.shape[0]
    scale = WIDTH ** (-0.5)
    per_half = HALF // SUB

    def place(block):
        return pl.multiple_of(order_ref[block] * HALF, HALF)

    for s in range(blocks):
        for half in range(2):
            rows = pl.ds(place(2 * s + half), HALF)
            lo = half * HALF
            q_s[rows, :NOPE] = in_ref[s, lo : lo + HALF, :]
            q_s[rows, NOPE:] = in_ref[s, ROW_ROPE:ROWS_IN, half * ROPE : (half + 1) * ROPE]
            d_s[rows, :] = in_ref[s, ROW_DO + lo : ROW_DO + lo + HALF, :]
    for shift in range(n_head):
        p = lax.rem(rank_ref[1] + n_head - shift, n_head)
        half, i = lax.div(p, per_half), lax.rem(p, per_half)
        for s in range(blocks):
            sub = pl.ds(pl.multiple_of(order_ref[2 * s + half] * HALF + i * SUB, SUB), SUB)
            lat_s[sub, :] = lat_refs[shift][s, :, :LAT]
            k_s[sub, NOPE:] = lat_refs[shift][s, :, LAT:]

    w_both = w_ref[...]
    for t in range(seq // TILE):
        rows = slice(t * TILE, (t + 1) * TILE)
        both = dot_nn(lat_s[rows, :], w_both)
        k_s[rows, :NOPE] = both[:, :NOPE].astype(BF)
        v_s[rows, :] = both[:, NOPE:].astype(BF)

    dk_s[...] = jnp.zeros_like(dk_s)
    dv_s[...] = jnp.zeros_like(dv_s)
    for t in range(seq // TILE):
        rows = slice(t * TILE, (t + 1) * TILE)
        width = (t + 1) * TILE
        q = q_s[rows, :]
        d = d_s[rows, :]
        k = k_s[:width, :]
        scores = dot_nt(k, q) * scale
        key_pos = lax.broadcasted_iota(jnp.int32, (width, TILE), 0)
        row_pos = lax.broadcasted_iota(jnp.int32, (width, TILE), 1) + t * TILE
        masked = jnp.where(key_pos <= row_pos, scores, -jnp.inf)
        top = jnp.max(masked, axis=0, keepdims=True)
        weights = jnp.exp(masked - top)
        probs = weights / jnp.sum(weights, axis=0, keepdims=True)
        probs_b = probs.astype(BF)
        dprob = dot_nt(v_s[:width, :], d)
        drow = jnp.sum(probs_b.astype(F32) * dprob, axis=0, keepdims=True)
        dscore = (probs * (dprob - drow)).astype(BF)
        dq_s[rows, :] = (dot_tn(dscore, k) * scale).astype(BF)
        dk_s[:width, :] += dot_nn(dscore, q)
        dv_s[:width, :] += dot_nn(probs_b, d)

    dk = dk_s[...] * scale
    dkv = jnp.concatenate([dk[:, :NOPE], dv_s[...]], axis=1).astype(BF)
    gw_s[...] = dot_tn(lat_s[...], dkv).astype(BF)
    share = LAT // n_dp
    for shift in range(n_dp):
        target = lax.rem(rank_ref[2] + shift, n_dp)
        gw_refs[shift][...] = gw_s[pl.ds(pl.multiple_of(target * share, share), share), :]
    gl_s[:, :LAT] = dot_nt(dkv, w_both).astype(BF)
    gl_s[:, LAT:] = dk[:, NOPE:].astype(BF)

    for s in range(blocks):
        for half in range(2):
            base = place(2 * s + half)
            rows = pl.ds(base, HALF)
            lo = half * HALF
            gq_ref[s, lo : lo + HALF, :] = dq_s[rows, :NOPE]
            gq_ref[s, ROW_GROPE:ROW_GL, half * ROPE : (half + 1) * ROPE] = dq_s[rows, NOPE:]
            for i in range(per_half):
                p = half * per_half + i
                sub = pl.ds(pl.multiple_of(base + i * SUB, SUB), SUB)
                for j in range(LAT // 128):
                    gl_ref[p, s, SUB * j : SUB * (j + 1), :] = gl_s[sub, 128 * j : 128 * (j + 1)]
                rope = gl_s[sub, LAT:]
                gl_ref[p, s, SUB * (LAT // 128) :, :] = jnp.concatenate([rope, rope], axis=1)


def combine_kernel(rank_ref, gq_ref, gl_ref, *out_refs):
    n_head, n_ctx = gl_ref.shape[:2]
    for shift in range(n_ctx):
        target = lax.rem(rank_ref[0] + shift, n_ctx)
        out_refs[shift][:ROW_GL, :] = gq_ref[target]
        total = gl_ref[0, target].astype(F32)
        for i in range(1, n_head):
            total = total + gl_ref[i, target].astype(F32)
        out_refs[shift][ROW_GL:, :] = total.astype(BF)


def unpack_kernel(n_ctx, rank_ref, *refs):
    part_refs, (gq_ref, gl_ref, in_s) = refs[:n_ctx], refs[n_ctx:]
    for shift in range(n_ctx):
        in_s[lax.rem(rank_ref[0] + n_ctx - shift, n_ctx)] = part_refs[shift][:ROW_GL, :]
    for h in range(n_ctx):
        rope = in_s[h, ROW_GROPE:ROW_GL, :]
        rope = jnp.concatenate([rope[:, :ROPE], rope[:, ROPE:]], axis=0)
        gq_ref[:, h * WIDTH : (h + 1) * WIDTH] = jnp.concatenate([in_s[h, :NOPE, :], rope], axis=1)
    total = part_refs[0][ROW_GL:, :].astype(F32)
    for i in range(1, n_ctx):
        total = total + part_refs[i][ROW_GL:, :].astype(F32)
    for j in range(LAT // 128):
        gl_ref[:, 128 * j : 128 * (j + 1)] = total[SUB * j : SUB * (j + 1)]
    gl_ref[:, LAT:] = total[SUB * (LAT // 128) :, :ROPE]


def assemble_kernel(group, rank_ref, in_ref, gk_ref, gv_ref):
    n_dp, n_ctx, share, _ = in_ref.shape
    for i, shift in enumerate(group):
        head = lax.rem(rank_ref[0] + n_ctx - shift, n_ctx)
        cols = pl.ds(pl.multiple_of(head * NOPE, NOPE), NOPE)
        for d in range(n_dp):
            part = in_ref[d, i].astype(F32)
            gk_ref[d * share : (d + 1) * share, cols] = part[:, :NOPE]
            gv_ref[d * share : (d + 1) * share, cols] = part[:, NOPE:]


def shifted(x, axis, n, shift):
    return lax.ppermute(x, axis, [(i, (i + shift) % n) for i in range(n)])


def whole(shape):
    return pl.BlockSpec(shape, lambda i, *scalars: (0,) * len(shape))


def call(kernel, name, scalars, inputs, outs, scratch=(), in_specs=None, flops=0, vmem=16):
    moved = sum(x.size * x.dtype.itemsize for x in inputs) + sum(
        x.size * x.dtype.itemsize for x in outs
    )
    return pl.pallas_call(
        kernel,
        grid_spec=pltpu.PrefetchScalarGridSpec(
            num_scalar_prefetch=len(scalars),
            grid=(1,),
            in_specs=in_specs or [whole(x.shape) for x in inputs],
            out_specs=[whole(x.shape) for x in outs],
            scratch_shapes=list(scratch),
        ),
        out_shape=list(outs),
        compiler_params=pltpu.CompilerParams(vmem_limit_bytes=vmem * 1024 * 1024),
        cost_estimate=pl.CostEstimate(flops=flops, bytes_accessed=moved, transcendentals=0),
        name=name,
    )(*scalars, *inputs)


def on_device(n_dp, n_ctx, n_head, query, latent, w_uk, w_uv, grad_out, block_order):
    seq = n_ctx * n_head * SUB
    rows = query.shape[1]
    shape = jax.ShapeDtypeStruct
    ranks = jnp.stack([lax.axis_index(a).astype(jnp.int32) for a in ("ctx", "head", "dp")])

    lat_mine = lax.all_to_all(
        jnp.broadcast_to(latent, (n_ctx, SUB, LAT + ROPE)), "ctx", 0, 0, tiled=True
    )
    lat_all = [lat_mine] + [shifted(lat_mine, "head", n_head, i) for i in range(1, n_head)]
    head_cols = pl.BlockSpec((LAT, NOPE), lambda i, rank: (0, rank[0]))
    packed, w_both = call(
        pack_kernel,
        "pack",
        (ranks,),
        (query[0], grad_out[0], w_uk, w_uv),
        [shape((n_ctx, ROWS_IN, 128), BF), shape((LAT, NOPE + VDIM), BF)],
        in_specs=[whole(query.shape[1:]), whole(grad_out.shape[1:]), head_cols, head_cols],
    )
    mine = lax.all_to_all(packed, "ctx", 0, 0, tiled=True)

    gl_part, gq_part, *gw_parts = call(
        functools.partial(attention_kernel, n_head, n_dp),
        "attention_backward",
        (block_order, ranks),
        (mine, w_both, *lat_all),
        [
            shape((n_head, n_ctx, SUB * (LAT // 128) + SUB, 128), BF),
            shape((n_ctx, ROW_GL, 128), BF),
        ]
        + [shape((LAT // n_dp, NOPE + VDIM), BF)] * n_dp,
        scratch=[
            pltpu.VMEM((seq, LAT), BF),
            pltpu.VMEM((seq, WIDTH), BF),
            pltpu.VMEM((seq, VDIM), BF),
            pltpu.VMEM((seq, WIDTH), BF),
            pltpu.VMEM((seq, VDIM), BF),
            pltpu.VMEM((seq, WIDTH), F32),
            pltpu.VMEM((seq, VDIM), F32),
            pltpu.VMEM((seq, WIDTH), BF),
            pltpu.VMEM((seq, LAT + ROPE), BF),
            pltpu.VMEM((LAT, NOPE + VDIM), BF),
        ],
        flops=3 * 10**9,
        vmem=28,
    )

    gw_sum = gw_parts[0].astype(F32)
    for i in range(1, n_dp):
        gw_sum = gw_sum + shifted(gw_parts[i], "dp", n_dp, i).astype(F32)
    gw_sum = gw_sum.astype(BF)
    group = [0, 1, n_ctx - 1] + list(range(2, n_ctx - 1))
    gw_ctx = jnp.stack([shifted(gw_sum, "ctx", n_ctx, i) if i else gw_sum for i in group])

    gl_moved = lax.all_to_all(gl_part, "head", 0, 0, tiled=True)
    gl_moved, gw_ctx = lax.optimization_barrier((gl_moved, gw_ctx))
    gw_all = lax.all_to_all(
        jnp.broadcast_to(gw_ctx[None], (n_dp,) + gw_ctx.shape), "dp", 0, 0, tiled=True
    )
    back = call(
        combine_kernel,
        "combine",
        (ranks,),
        (gq_part, gl_moved),
        [shape((ROWS_OUT, 128), BF)] * n_ctx,
    )
    back = [back[0]] + [shifted(back[i], "ctx", n_ctx, i) for i in range(1, n_ctx)]
    grad_query, grad_latent = call(
        functools.partial(unpack_kernel, n_ctx),
        "unpack",
        (ranks,),
        back,
        [shape((rows, n_ctx * WIDTH), BF), shape((SUB, LAT + ROPE), F32)],
        scratch=[pltpu.VMEM((n_ctx, ROW_GL, 128), BF)],
    )
    grad_query, grad_latent, gw_all = lax.optimization_barrier((grad_query, grad_latent, gw_all))
    grad_w_uk, grad_w_uv = call(
        functools.partial(assemble_kernel, group),
        "assemble",
        (ranks,),
        (gw_all,),
        [shape((LAT, n_ctx * NOPE), F32), shape((LAT, n_ctx * VDIM), F32)],
    )
    return (grad_query[None], grad_latent[None], grad_w_uk, grad_w_uv)


def solution(mesh):
    sizes = mesh.shape
    return jax.shard_map(
        functools.partial(on_device, sizes["dp"], sizes["ctx"], sizes["head"]),
        mesh=mesh,
        in_specs=(
            P("dp", "ctx", "head"),
            P("dp", ("ctx", "head"), None),
            P(None, "head"),
            P(None, "head"),
            P("dp", "ctx", "head"),
            P(),
        ),
        out_specs=(
            P("dp", "ctx", "head"),
            P("dp", ("ctx", "head"), None),
            P(None, "head"),
            P(None, "head"),
        ),
        check_vma=False,
    )
```

```python
import functools

import jax
import jax.numpy as jnp
from jax import lax
from jax.experimental import pallas as pl
from jax.experimental.pallas import tpu as pltpu
from jax.sharding import PartitionSpec as P

LAT = 512
ROPE = 64
NOPE = 128
VDIM = 128
WIDTH = NOPE + ROPE
HALF = 64
SUB = 16
TILE = 256
BF = jnp.bfloat16
F32 = jnp.float32
VMEM = pl.BlockSpec(memory_space=pltpu.VMEM)

ROW_DO = NOPE
ROW_ROPE = ROW_DO + VDIM
ROWS_IN = ROW_ROPE + ROPE
ROW_GROPE = NOPE
ROW_GL = ROW_GROPE + ROPE
ROW_GLROPE = ROW_GL + SUB * (LAT // 128)
ROWS_OUT = ROW_GLROPE + SUB


def dot_nn(a, b):
    return lax.dot_general(a, b, (((1,), (0,)), ((), ())), preferred_element_type=F32)


def dot_nt(a, b):
    return lax.dot_general(a, b, (((1,), (1,)), ((), ())), preferred_element_type=F32)


def dot_tn(a, b):
    return lax.dot_general(a, b, (((0,), (0,)), ((), ())), preferred_element_type=F32)


def pack_kernel(rank_ref, q_ref, d_ref, wk_ref, wv_ref, out_ref, w_ref):
    n = out_ref.shape[0]
    for h in range(n):
        q = q_ref[:, h * WIDTH : (h + 1) * WIDTH]
        out_ref[h, 0:ROW_DO, :] = q[:, :NOPE]
        out_ref[h, ROW_DO:ROW_ROPE, :] = d_ref[:, h * VDIM : (h + 1) * VDIM]
        rope = q[:, NOPE:]
        out_ref[h, ROW_ROPE:ROWS_IN, :] = jnp.concatenate([rope[:HALF], rope[HALF:]], axis=1)
    w_ref[:, :NOPE] = wk_ref[...]
    w_ref[:, NOPE:] = wv_ref[...]


def attention_kernel(n_head, n_dp, order_ref, rank_ref, in_ref, w_ref, *refs):
    lat_refs, refs = refs[:n_head], refs[n_head:]
    gl_refs, gw_refs, gq_ref = refs[:2], refs[2 : 2 + n_dp], refs[2 + n_dp]
    lat_s, k_s, v_s, q_s, d_s, dk_s, dv_s, dq_s, gl_s, gw_s = refs[3 + n_dp :]
    blocks = in_ref.shape[0]
    seq = lat_s.shape[0]
    scale = WIDTH ** (-0.5)
    per_half = HALF // SUB

    def place(block):
        return pl.multiple_of(order_ref[block] * HALF, HALF)

    for s in range(blocks):
        for half in range(2):
            rows = pl.ds(place(2 * s + half), HALF)
            lo = half * HALF
            q_s[rows, :NOPE] = in_ref[s, lo : lo + HALF, :]
            q_s[rows, NOPE:] = in_ref[s, ROW_ROPE:ROWS_IN, half * ROPE : (half + 1) * ROPE]
            d_s[rows, :] = in_ref[s, ROW_DO + lo : ROW_DO + lo + HALF, :]
    for shift in range(n_head):
        p = lax.rem(rank_ref[1] + n_head - shift, n_head)
        half, i = lax.div(p, per_half), lax.rem(p, per_half)
        for s in range(blocks):
            sub = pl.ds(pl.multiple_of(order_ref[2 * s + half] * HALF + i * SUB, SUB), SUB)
            lat_s[sub, :] = lat_refs[shift][s, :, :LAT]
            k_s[sub, NOPE:] = lat_refs[shift][s, :, LAT:]

    w_both = w_ref[...]
    for t in range(seq // TILE):
        rows = slice(t * TILE, (t + 1) * TILE)
        both = dot_nn(lat_s[rows, :], w_both)
        k_s[rows, :NOPE] = both[:, :NOPE].astype(BF)
        v_s[rows, :] = both[:, NOPE:].astype(BF)

    dk_s[...] = jnp.zeros_like(dk_s)
    dv_s[...] = jnp.zeros_like(dv_s)
    for t in range(seq // TILE):
        rows = slice(t * TILE, (t + 1) * TILE)
        width = (t + 1) * TILE
        q = q_s[rows, :]
        d = d_s[rows, :]
        k = k_s[:width, :]
        scores = dot_nt(k, q) * scale
        key_pos = lax.broadcasted_iota(jnp.int32, (width, TILE), 0)
        row_pos = lax.broadcasted_iota(jnp.int32, (width, TILE), 1) + t * TILE
        masked = jnp.where(key_pos <= row_pos, scores, -jnp.inf)
        top = jnp.max(masked, axis=0, keepdims=True)
        weights = jnp.exp(masked - top)
        probs = weights / jnp.sum(weights, axis=0, keepdims=True)
        probs_b = probs.astype(BF)
        dprob = dot_nt(v_s[:width, :], d)
        drow = jnp.sum(probs_b.astype(F32) * dprob, axis=0, keepdims=True)
        dscore = (probs * (dprob - drow)).astype(BF)
        dq_s[rows, :] = (dot_tn(dscore, k) * scale).astype(BF)
        dk_s[:width, :] += dot_nn(dscore, q)
        dv_s[:width, :] += dot_nn(probs_b, d)

    dk = dk_s[...] * scale
    dkv = jnp.concatenate([dk[:, :NOPE], dv_s[...]], axis=1).astype(BF)
    gw_s[...] = dot_tn(lat_s[...], dkv).astype(BF)
    share = LAT // n_dp
    for shift in range(n_dp):
        target = lax.rem(rank_ref[2] + shift, n_dp)
        gw_refs[shift][...] = gw_s[pl.ds(pl.multiple_of(target * share, share), share), :]
    gl_s[:, :LAT] = dot_nt(dkv, w_both).astype(BF)
    gl_s[:, LAT:] = dk[:, NOPE:].astype(BF)

    for s in range(blocks):
        for half in range(2):
            base = place(2 * s + half)
            rows = pl.ds(base, HALF)
            lo = half * HALF
            gq_ref[s, lo : lo + HALF, :] = dq_s[rows, :NOPE]
            gq_ref[s, ROW_GROPE:ROW_GL, half * ROPE : (half + 1) * ROPE] = dq_s[rows, NOPE:]
    n_x = n_head // 2
    x, core = lax.div(rank_ref[1], 2), lax.rem(rank_ref[1], 2)
    for flip in range(2):
        for shift in range(n_x):
            p = lax.rem(x + shift, n_x) * 2 + lax.rem(core + flip, 2)
            half, i = lax.div(p, per_half), lax.rem(p, per_half)
            for s in range(blocks):
                sub = pl.ds(pl.multiple_of(order_ref[2 * s + half] * HALF + i * SUB, SUB), SUB)
                out_ref = gl_refs[flip].at[shift, s]
                for j in range(LAT // 128):
                    out_ref[SUB * j : SUB * (j + 1), :] = gl_s[sub, 128 * j : 128 * (j + 1)]
                rope = gl_s[sub, LAT:]
                out_ref[SUB * (LAT // 128) :, :] = jnp.concatenate([rope, rope], axis=1)


def fold_kernel(keep_ref, moved_ref, *out_refs):
    for shift, out_ref in enumerate(out_refs):
        out_ref[...] = (keep_ref[shift].astype(F32) + moved_ref[shift].astype(F32)).astype(BF)


def combine_kernel(gq_ref, *refs):
    gl_refs, out_ref = refs[:-1], refs[-1]
    out_ref[:, :ROW_GL, :] = gq_ref[...]
    total = gl_refs[0][...].astype(F32)
    for gl_ref in gl_refs[1:]:
        total = total + gl_ref[...].astype(F32)
    out_ref[:, ROW_GL:, :] = total.astype(BF)


def unpack_kernel(in_ref, gq_ref, gl_ref):
    n = in_ref.shape[0]
    for h in range(n):
        rope = in_ref[h, ROW_GROPE:ROW_GL, :]
        rope = jnp.concatenate([rope[:, :ROPE], rope[:, ROPE:]], axis=0)
        gq_ref[:, h * WIDTH : (h + 1) * WIDTH] = jnp.concatenate([in_ref[h, :NOPE, :], rope], axis=1)
    for j in range(LAT // 128):
        part = in_ref[:, ROW_GL + SUB * j : ROW_GL + SUB * (j + 1), :].astype(F32)
        gl_ref[:, 128 * j : 128 * (j + 1)] = jnp.sum(part, axis=0)
    part = in_ref[:, ROW_GLROPE:ROWS_OUT, :ROPE].astype(F32)
    gl_ref[:, LAT:] = jnp.sum(part, axis=0)


def assemble_kernel(n_dp, rank_ref, *refs):
    in_refs, (gk_ref, gv_ref) = refs[:-2], refs[-2:]
    share = in_refs[0].shape[1]
    half = in_refs[3].shape[0]
    for in_ref, step, first in zip(in_refs, (0, 3, 1, 2, 2), (0, 0, 0, 0, half)):
        source = lax.rem(rank_ref[2] + step, n_dp)
        rows = pl.ds(pl.multiple_of(source * share, share), share)
        for i in range(in_ref.shape[0]):
            h = first + i
            part = in_ref[i].astype(F32)
            gk_ref[rows, h * NOPE : (h + 1) * NOPE] = part[:, :NOPE]
            gv_ref[rows, h * VDIM : (h + 1) * VDIM] = part[:, NOPE:]


def shifted(x, axis, n, shift):
    return lax.ppermute(x, axis, [(i, (i + shift) % n) for i in range(n)])


def whole(shape):
    return pl.BlockSpec(shape, lambda i, *scalars: (0,) * len(shape))


def call(kernel, name, scalars, inputs, outs, scratch=(), in_specs=None, flops=0, vmem=16):
    moved = sum(x.size * x.dtype.itemsize for x in inputs) + sum(
        x.size * x.dtype.itemsize for x in outs
    )
    return pl.pallas_call(
        kernel,
        grid_spec=pltpu.PrefetchScalarGridSpec(
            num_scalar_prefetch=len(scalars),
            grid=(1,),
            in_specs=in_specs or [whole(x.shape) for x in inputs],
            out_specs=[whole(x.shape) for x in outs],
            scratch_shapes=list(scratch),
        ),
        out_shape=list(outs),
        compiler_params=pltpu.CompilerParams(vmem_limit_bytes=vmem * 1024 * 1024),
        cost_estimate=pl.CostEstimate(flops=flops, bytes_accessed=moved, transcendentals=0),
        name=name,
    )(*scalars, *inputs)


def on_device(n_dp, n_ctx, n_head, query, latent, w_uk, w_uv, grad_out, block_order):
    seq = n_ctx * n_head * SUB
    rows = query.shape[1]
    shape = jax.ShapeDtypeStruct
    ranks = jnp.stack([lax.axis_index(a).astype(jnp.int32) for a in ("ctx", "head", "dp")])

    lat_mine = lax.all_to_all(
        jnp.broadcast_to(latent, (n_ctx, SUB, LAT + ROPE)), "ctx", 0, 0, tiled=True
    )
    lat_all = [lat_mine] + [shifted(lat_mine, "head", n_head, i) for i in range(1, n_head)]
    head_cols = pl.BlockSpec((LAT, NOPE), lambda i, rank: (0, rank[0]))
    packed, w_both = call(
        pack_kernel,
        "pack",
        (ranks,),
        (query[0], grad_out[0], w_uk, w_uv),
        [shape((n_ctx, ROWS_IN, 128), BF), shape((LAT, NOPE + VDIM), BF)],
        in_specs=[whole(query.shape[1:]), whole(grad_out.shape[1:]), head_cols, head_cols],
    )
    mine = lax.all_to_all(packed, "ctx", 0, 0, tiled=True)

    gl_keep, gl_send, *gw_parts, gq_part = call(
        functools.partial(attention_kernel, n_head, n_dp),
        "attention_backward",
        (block_order, ranks),
        (mine, w_both, *lat_all),
        [shape((n_head // 2, n_ctx, SUB * (LAT // 128) + SUB, 128), BF)] * 2
        + [shape((LAT // n_dp, NOPE + VDIM), BF)] * n_dp
        + [shape((n_ctx, ROW_GL, 128), BF)],
        scratch=[
            pltpu.VMEM((seq, LAT), BF),
            pltpu.VMEM((seq, WIDTH), BF),
            pltpu.VMEM((seq, VDIM), BF),
            pltpu.VMEM((seq, WIDTH), BF),
            pltpu.VMEM((seq, VDIM), BF),
            pltpu.VMEM((seq, WIDTH), F32),
            pltpu.VMEM((seq, VDIM), F32),
            pltpu.VMEM((seq, WIDTH), BF),
            pltpu.VMEM((seq, LAT + ROPE), BF),
            pltpu.VMEM((LAT, NOPE + VDIM), BF),
        ],
        flops=3 * 10**9,
        vmem=28,
    )

    gw_sum = gw_parts[0].astype(F32)
    for i in range(1, n_dp):
        gw_sum = gw_sum + shifted(gw_parts[i], "dp", n_dp, i).astype(F32)
    gw_sum = gw_sum.astype(BF)
    flip = [(i, i ^ 1) for i in range(n_head)]
    gl_recv = lax.ppermute(gl_send, "head", flip)
    gw_sum, gl_recv = lax.optimization_barrier((gw_sum, gl_recv))
    folded = call(
        fold_kernel,
        "fold",
        (),
        (gl_keep, gl_recv),
        [shape(gl_keep.shape[1:], BF)] * (n_head // 2),
    )
    gw_ctx = lax.all_to_all(
        jnp.broadcast_to(gw_sum[None], (n_ctx,) + gw_sum.shape), "ctx", 0, 0, tiled=True
    )
    gl_moved = [folded[0]] + [
        lax.ppermute(folded[i], "head", [(j, (j + 2 * i) % n_head) for j in range(n_head)])
        for i in range(1, n_head // 2)
    ]
    gw_ctx, *gl_moved = lax.optimization_barrier((gw_ctx, *gl_moved))
    half = n_ctx // 2
    before, after = shifted(gw_ctx, "dp", n_dp, 1), shifted(gw_ctx, "dp", n_dp, n_dp - 1)
    gw_all = [
        gw_ctx,
        before,
        after,
        shifted(before[:half], "dp", n_dp, 1),
        shifted(after[half:], "dp", n_dp, n_dp - 1),
    ]
    back = call(
        combine_kernel,
        "combine",
        (),
        (gq_part, *gl_moved),
        [shape((n_ctx, ROWS_OUT, 128), BF)],
    )[0]
    back = lax.all_to_all(back, "ctx", 0, 0, tiled=True)
    grad_query, grad_latent = call(
        unpack_kernel,
        "unpack",
        (),
        (back,),
        [shape((rows, n_ctx * WIDTH), BF), shape((SUB, LAT + ROPE), F32)],
    )
    grad_query, grad_latent, *gw_all = lax.optimization_barrier((grad_query, grad_latent, *gw_all))
    grad_w_uk, grad_w_uv = call(
        functools.partial(assemble_kernel, n_dp),
        "assemble",
        (ranks,),
        gw_all,
        [shape((LAT, n_ctx * NOPE), F32), shape((LAT, n_ctx * VDIM), F32)],
    )
    return (grad_query[None], grad_latent[None], grad_w_uk, grad_w_uv)


def solution(mesh):
    sizes = mesh.shape
    return jax.shard_map(
        functools.partial(on_device, sizes["dp"], sizes["ctx"], sizes["head"]),
        mesh=mesh,
        in_specs=(
            P("dp", "ctx", "head"),
            P("dp", ("ctx", "head"), None),
            P(None, "head"),
            P(None, "head"),
            P("dp", "ctx", "head"),
            P(),
        ),
        out_specs=(
            P("dp", "ctx", "head"),
            P("dp", ("ctx", "head"), None),
            P(None, "head"),
            P(None, "head"),
        ),
        check_vma=False,
    )
```

```python
import functools

import jax
import jax.numpy as jnp
from jax import lax
from jax.experimental import pallas as pl
from jax.experimental.pallas import tpu as pltpu
from jax.sharding import PartitionSpec as P

LAT = 512
ROPE = 64
NOPE = 128
VDIM = 128
WIDTH = NOPE + ROPE
HALF = 64
SUB = 16
TILE = 256
BF = jnp.bfloat16
F32 = jnp.float32
ANY = pl.BlockSpec(memory_space=pl.ANY)

ROW_DO = NOPE
ROW_ROPE = ROW_DO + VDIM
ROWS_IN = ROW_ROPE + ROPE
ROW_GROPE = NOPE
ROW_GL = ROW_GROPE + ROPE
ROW_GLROPE = ROW_GL + SUB * (LAT // 128)
ROWS_OUT = ROW_GLROPE + SUB


def dot_nn(a, b):
    return lax.dot_general(a, b, (((1,), (0,)), ((), ())), preferred_element_type=F32)


def dot_nt(a, b):
    return lax.dot_general(a, b, (((1,), (1,)), ((), ())), preferred_element_type=F32)


def dot_tn(a, b):
    return lax.dot_general(a, b, (((0,), (0,)), ((), ())), preferred_element_type=F32)


def pack_kernel(rank_ref, q_ref, d_ref, wk_ref, wv_ref, out_ref, w_ref):
    n = out_ref.shape[0]
    for h in range(n):
        q = q_ref[:, h * WIDTH : (h + 1) * WIDTH]
        out_ref[h, 0:ROW_DO, :] = q[:, :NOPE]
        out_ref[h, ROW_DO:ROW_ROPE, :] = d_ref[:, h * VDIM : (h + 1) * VDIM]
        rope = q[:, NOPE:]
        out_ref[h, ROW_ROPE:ROWS_IN, :] = jnp.concatenate([rope[:HALF], rope[HALF:]], axis=1)
    w_ref[:, :NOPE] = wk_ref[...]
    w_ref[:, NOPE:] = wv_ref[...]


def attention_kernel(n_head, n_dp, order_ref, rank_ref, in_ref, w_ref, *refs):
    lat_refs, refs = refs[:n_head], refs[n_head:]
    gl_refs, gw_refs, gq_ref = refs[:2], refs[2 : 2 + n_dp], refs[2 + n_dp]
    lat_s, k_s, v_s, q_s, d_s, dk_s, dv_s, dq_s, gl_s, gw_s = refs[3 + n_dp :]
    blocks = in_ref.shape[0]
    seq = lat_s.shape[0]
    scale = WIDTH ** (-0.5)
    per_half = HALF // SUB
    n_x = n_head // 2
    x, core = lax.div(rank_ref[1], 2), lax.rem(rank_ref[1], 2)

    def place(block):
        return pl.multiple_of(order_ref[block] * HALF, HALF)

    for s in range(blocks):
        for half in range(2):
            rows = pl.ds(place(2 * s + half), HALF)
            lo = half * HALF
            q_s[rows, :NOPE] = in_ref[s, lo : lo + HALF, :]
            q_s[rows, NOPE:] = in_ref[s, ROW_ROPE:ROWS_IN, half * ROPE : (half + 1) * ROPE]
            d_s[rows, :] = in_ref[s, ROW_DO + lo : ROW_DO + lo + HALF, :]
    for shift in range(n_head):
        other, back = divmod(shift, n_x)
        p = lax.rem(x + n_x - back, n_x) * 2 + lax.rem(core + other, 2)
        half, i = lax.div(p, per_half), lax.rem(p, per_half)
        for s in range(blocks):
            sub = pl.ds(pl.multiple_of(order_ref[2 * s + half] * HALF + i * SUB, SUB), SUB)
            lat_s[sub, :] = lat_refs[shift][s, :, :LAT]
            k_s[sub, NOPE:] = lat_refs[shift][s, :, LAT:]

    w_both = w_ref[...]
    for t in range(seq // TILE):
        rows = slice(t * TILE, (t + 1) * TILE)
        both = dot_nn(lat_s[rows, :], w_both)
        k_s[rows, :NOPE] = both[:, :NOPE].astype(BF)
        v_s[rows, :] = both[:, NOPE:].astype(BF)

    dk_s[...] = jnp.zeros_like(dk_s)
    dv_s[...] = jnp.zeros_like(dv_s)
    for t in range(seq // TILE):
        rows = slice(t * TILE, (t + 1) * TILE)
        width = (t + 1) * TILE
        q = q_s[rows, :]
        d = d_s[rows, :]
        k = k_s[:width, :]
        scores = dot_nt(k, q) * scale
        key_pos = lax.broadcasted_iota(jnp.int32, (width, TILE), 0)
        row_pos = lax.broadcasted_iota(jnp.int32, (width, TILE), 1) + t * TILE
        masked = jnp.where(key_pos <= row_pos, scores, -jnp.inf)
        top = jnp.max(masked, axis=0, keepdims=True)
        weights = jnp.exp(masked - top)
        probs = weights / jnp.sum(weights, axis=0, keepdims=True)
        probs_b = probs.astype(BF)
        dprob = dot_nt(v_s[:width, :], d)
        drow = jnp.sum(probs_b.astype(F32) * dprob, axis=0, keepdims=True)
        dscore = (probs * (dprob - drow)).astype(BF)
        dq_s[rows, :] = (dot_tn(dscore, k) * scale).astype(BF)
        dk_s[:width, :] += dot_nn(dscore, q)
        dv_s[:width, :] += dot_nn(probs_b, d)

    dk = dk_s[...] * scale
    dkv = jnp.concatenate([dk[:, :NOPE], dv_s[...]], axis=1).astype(BF)
    gw_s[...] = dot_tn(lat_s[...], dkv).astype(BF)
    share = LAT // n_dp
    for shift in range(n_dp):
        target = lax.rem(rank_ref[2] + shift, n_dp)
        gw_refs[shift][...] = gw_s[pl.ds(pl.multiple_of(target * share, share), share), :]
    gl_s[:, :LAT] = dot_nt(dkv, w_both).astype(BF)
    gl_s[:, LAT:] = dk[:, NOPE:].astype(BF)

    for s in range(blocks):
        for half in range(2):
            base = place(2 * s + half)
            rows = pl.ds(base, HALF)
            lo = half * HALF
            gq_ref[s, lo : lo + HALF, :] = dq_s[rows, :NOPE]
            gq_ref[s, ROW_GROPE:ROW_GL, half * ROPE : (half + 1) * ROPE] = dq_s[rows, NOPE:]
    for flip in range(2):
        for shift in range(n_x):
            p = lax.rem(x + shift, n_x) * 2 + lax.rem(core + flip, 2)
            half, i = lax.div(p, per_half), lax.rem(p, per_half)
            for s in range(blocks):
                sub = pl.ds(pl.multiple_of(order_ref[2 * s + half] * HALF + i * SUB, SUB), SUB)
                out_ref = gl_refs[flip].at[shift, s]
                for j in range(LAT // 128):
                    out_ref[SUB * j : SUB * (j + 1), :] = gl_s[sub, 128 * j : 128 * (j + 1)]
                rope = gl_s[sub, LAT:]
                out_ref[SUB * (LAT // 128) :, :] = jnp.concatenate([rope, rope], axis=1)


def fold_kernel(keep_ref, moved_ref, *out_refs):
    for shift, out_ref in enumerate(out_refs):
        out_ref[...] = (keep_ref[shift].astype(F32) + moved_ref[shift].astype(F32)).astype(BF)


def combine_kernel(gq_ref, *refs):
    gl_refs, out_ref = refs[:-1], refs[-1]
    out_ref[:, :ROW_GL, :] = gq_ref[...]
    total = gl_refs[0][...].astype(F32)
    for gl_ref in gl_refs[1:]:
        total = total + gl_ref[...].astype(F32)
    out_ref[:, ROW_GL:, :] = total.astype(BF)


def unpack_kernel(in_ref, gq_ref, gl_ref):
    n = in_ref.shape[0]
    for h in range(n):
        rope = in_ref[h, ROW_GROPE:ROW_GL, :]
        rope = jnp.concatenate([rope[:, :ROPE], rope[:, ROPE:]], axis=0)
        gq_ref[:, h * WIDTH : (h + 1) * WIDTH] = jnp.concatenate([in_ref[h, :NOPE, :], rope], axis=1)
    for j in range(LAT // 128):
        part = in_ref[:, ROW_GL + SUB * j : ROW_GL + SUB * (j + 1), :].astype(F32)
        gl_ref[:, 128 * j : 128 * (j + 1)] = jnp.sum(part, axis=0)
    part = in_ref[:, ROW_GLROPE:ROWS_OUT, :ROPE].astype(F32)
    gl_ref[:, LAT:] = jnp.sum(part, axis=0)


def assemble_kernel(steps, n_dp, rank_ref, *refs):
    n_in = sum(len(group) for group in steps.values())
    in_refs = list(refs[:n_in])
    gk_ref, gv_ref, gk_s, gv_s, sems = refs[-5:]
    share = in_refs[0].shape[1]
    copies = []
    for k, (step, group) in enumerate(steps.items()):
        h = 0
        for in_ref in [in_refs[i] for i in group]:
            for i in range(in_ref.shape[0]):
                part = in_ref[i].astype(F32)
                gk_s[k, :, h * NOPE : (h + 1) * NOPE] = part[:, :NOPE]
                gv_s[k, :, h * VDIM : (h + 1) * VDIM] = part[:, NOPE:]
                h += 1
        source = lax.rem(rank_ref[2] + n_dp - step, n_dp)
        rows = pl.ds(pl.multiple_of(source * share, share), share)
        copies.append(pltpu.make_async_copy(gk_s.at[k], gk_ref.at[rows], sems.at[k, 0]))
        copies.append(pltpu.make_async_copy(gv_s.at[k], gv_ref.at[rows], sems.at[k, 1]))
        copies[-2].start()
        copies[-1].start()
    for copy in copies:
        copy.wait()


def assemble(name, steps, n_dp, ranks, parts, outs, filled=()):
    n, rows = len(steps), parts[0].shape[1]
    return call(
        functools.partial(assemble_kernel, steps, n_dp),
        name,
        (ranks,),
        (*parts, *filled),
        outs,
        scratch=[pltpu.VMEM((n, rows, outs[i].shape[1]), F32) for i in range(2)]
        + [pltpu.SemaphoreType.DMA((n, 2))],
        in_specs=[whole(part.shape) for part in parts] + [ANY] * len(filled),
        out_specs=[ANY, ANY],
        aliases={1 + len(parts) + i: i for i in range(len(filled))},
    )


def shifted(x, axis, n, shift):
    return lax.ppermute(x, axis, [(i, (i + shift) % n) for i in range(n)])


def whole(shape):
    return pl.BlockSpec(shape, lambda i, *scalars: (0,) * len(shape))


def call(
    kernel, name, scalars, inputs, outs, scratch=(), in_specs=None, flops=0, vmem=16,
    out_specs=None, aliases=None,
):
    moved = sum(x.size * x.dtype.itemsize for x in inputs) + sum(
        x.size * x.dtype.itemsize for x in outs
    )
    return pl.pallas_call(
        kernel,
        grid_spec=pltpu.PrefetchScalarGridSpec(
            num_scalar_prefetch=len(scalars),
            grid=(1,),
            in_specs=in_specs or [whole(x.shape) for x in inputs],
            out_specs=out_specs or [whole(x.shape) for x in outs],
            scratch_shapes=list(scratch),
        ),
        out_shape=list(outs),
        input_output_aliases=aliases or {},
        compiler_params=pltpu.CompilerParams(vmem_limit_bytes=vmem * 1024 * 1024),
        cost_estimate=pl.CostEstimate(flops=flops, bytes_accessed=moved, transcendentals=0),
        name=name,
    )(*scalars, *inputs)


def on_device(n_dp, n_ctx, n_head, query, latent, w_uk, w_uv, grad_out, block_order):
    seq = n_ctx * n_head * SUB
    rows = query.shape[1]
    shape = jax.ShapeDtypeStruct
    ranks = jnp.stack([lax.axis_index(a).astype(jnp.int32) for a in ("ctx", "head", "dp")])

    lat_mine = lax.all_to_all(
        jnp.broadcast_to(latent, (n_ctx, SUB, LAT + ROPE)), "ctx", 0, 0, tiled=True
    )
    flip = [(i, i ^ 1) for i in range(n_head)]
    lat_all = [lat_mine] + [shifted(lat_mine, "head", n_head, 2 * i) for i in range(1, n_head // 2)]
    lat_all += [lax.ppermute(part, "head", flip) for part in lat_all]
    head_cols = pl.BlockSpec((LAT, NOPE), lambda i, rank: (0, rank[0]))
    packed, w_both = call(
        pack_kernel,
        "pack",
        (ranks,),
        (query[0], grad_out[0], w_uk, w_uv),
        [shape((n_ctx, ROWS_IN, 128), BF), shape((LAT, NOPE + VDIM), BF)],
        in_specs=[whole(query.shape[1:]), whole(grad_out.shape[1:]), head_cols, head_cols],
    )
    mine = lax.all_to_all(packed, "ctx", 0, 0, tiled=True)

    gl_keep, gl_send, *gw_parts, gq_part = call(
        functools.partial(attention_kernel, n_head, n_dp),
        "attention_backward",
        (block_order, ranks),
        (mine, w_both, *lat_all),
        [shape((n_head // 2, n_ctx, SUB * (LAT // 128) + SUB, 128), BF)] * 2
        + [shape((LAT // n_dp, NOPE + VDIM), BF)] * n_dp
        + [shape((n_ctx, ROW_GL, 128), BF)],
        scratch=[
            pltpu.VMEM((seq, LAT), BF),
            pltpu.VMEM((seq, WIDTH), BF),
            pltpu.VMEM((seq, VDIM), BF),
            pltpu.VMEM((seq, WIDTH), BF),
            pltpu.VMEM((seq, VDIM), BF),
            pltpu.VMEM((seq, WIDTH), F32),
            pltpu.VMEM((seq, VDIM), F32),
            pltpu.VMEM((seq, WIDTH), BF),
            pltpu.VMEM((seq, LAT + ROPE), BF),
            pltpu.VMEM((LAT, NOPE + VDIM), BF),
        ],
        flops=3 * 10**9,
        vmem=28,
    )

    gw_sum = gw_parts[0].astype(F32)
    for i in range(1, n_dp):
        gw_sum = gw_sum + shifted(gw_parts[i], "dp", n_dp, i).astype(F32)
    gw_sum = gw_sum.astype(BF)
    gl_recv = lax.ppermute(gl_send, "head", flip)
    gw_sum, gl_recv = lax.optimization_barrier((gw_sum, gl_recv))
    folded = call(
        fold_kernel,
        "fold",
        (),
        (gl_keep, gl_recv),
        [shape(gl_keep.shape[1:], BF)] * (n_head // 2),
    )
    gw_ctx = lax.all_to_all(
        jnp.broadcast_to(gw_sum[None], (n_ctx,) + gw_sum.shape), "ctx", 0, 0, tiled=True
    )
    gl_moved = [folded[0]] + [
        lax.ppermute(folded[i], "head", [(j, (j + 2 * i) % n_head) for j in range(n_head)])
        for i in range(1, n_head // 2)
    ]
    gw_ctx, *gl_moved = lax.optimization_barrier((gw_ctx, *gl_moved))
    half = n_ctx // 2
    before, after = shifted(gw_ctx, "dp", n_dp, 1), shifted(gw_ctx, "dp", n_dp, n_dp - 1)
    opposite = [
        shifted(before[:half], "dp", n_dp, 1),
        shifted(after[half:], "dp", n_dp, n_dp - 1),
    ]
    back = call(
        combine_kernel,
        "combine",
        (),
        (gq_part, *gl_moved),
        [shape((n_ctx, ROWS_OUT, 128), BF)],
    )[0]
    back = lax.all_to_all(back, "ctx", 0, 0, tiled=True)
    grad_query, grad_latent = call(
        unpack_kernel,
        "unpack",
        (),
        (back,),
        [shape((rows, n_ctx * WIDTH), BF), shape((SUB, LAT + ROPE), F32)],
    )
    outs = [shape((LAT, n_ctx * NOPE), F32), shape((LAT, n_ctx * VDIM), F32)]
    filled = assemble(
        "assemble_near", {0: [0], 1: [1], 3: [2]}, n_dp, ranks, [gw_ctx, before, after], outs
    )
    grad_query, grad_latent, *opposite = lax.optimization_barrier(
        (grad_query, grad_latent, *opposite)
    )
    grad_w_uk, grad_w_uv = assemble(
        "assemble_far", {2: [0, 1]}, n_dp, ranks, opposite, outs, filled
    )
    return (grad_query[None], grad_latent[None], grad_w_uk, grad_w_uv)


def solution(mesh):
    sizes = mesh.shape
    return jax.shard_map(
        functools.partial(on_device, sizes["dp"], sizes["ctx"], sizes["head"]),
        mesh=mesh,
        in_specs=(
            P("dp", "ctx", "head"),
            P("dp", ("ctx", "head"), None),
            P(None, "head"),
            P(None, "head"),
            P("dp", "ctx", "head"),
            P(),
        ),
        out_specs=(
            P("dp", "ctx", "head"),
            P("dp", ("ctx", "head"), None),
            P(None, "head"),
            P(None, "head"),
        ),
        check_vma=False,
    )
```

```python
import functools

import jax
import jax.numpy as jnp
from jax import lax
from jax.experimental import pallas as pl
from jax.experimental.pallas import tpu as pltpu
from jax.sharding import PartitionSpec as P

LAT = 512
ROPE = 64
NOPE = 128
VDIM = 128
WIDTH = NOPE + ROPE
HALF = 64
SUB = 16
TILE = 256
BF = jnp.bfloat16
F32 = jnp.float32
ANY = pl.BlockSpec(memory_space=pl.ANY)

ROW_DO = NOPE
ROW_ROPE = ROW_DO + VDIM
ROWS_IN = ROW_ROPE + ROPE
ROW_GROPE = NOPE
ROW_GL = ROW_GROPE + ROPE
ROW_GLROPE = ROW_GL + SUB * (LAT // 128)
ROWS_OUT = ROW_GLROPE + SUB


def dot_nn(a, b):
    return lax.dot_general(a, b, (((1,), (0,)), ((), ())), preferred_element_type=F32)


def dot_nt(a, b):
    return lax.dot_general(a, b, (((1,), (1,)), ((), ())), preferred_element_type=F32)


def dot_tn(a, b):
    return lax.dot_general(a, b, (((0,), (0,)), ((), ())), preferred_element_type=F32)


def pack_kernel(rank_ref, q_ref, d_ref, wk_ref, wv_ref, out_ref, w_ref):
    n = out_ref.shape[0]
    for h in range(n):
        q = q_ref[:, h * WIDTH : (h + 1) * WIDTH]
        out_ref[h, 0:ROW_DO, :] = q[:, :NOPE]
        out_ref[h, ROW_DO:ROW_ROPE, :] = d_ref[:, h * VDIM : (h + 1) * VDIM]
        rope = q[:, NOPE:]
        out_ref[h, ROW_ROPE:ROWS_IN, :] = jnp.concatenate([rope[:HALF], rope[HALF:]], axis=1)
    w_ref[:, :NOPE] = wk_ref[...]
    w_ref[:, NOPE:] = wv_ref[...]


def attention_kernel(n_head, n_dp, order_ref, rank_ref, in_ref, w_ref, *refs):
    lat_refs, refs = refs[:n_head], refs[n_head:]
    gl_refs, gw_refs, gq_ref = refs[:2], refs[2 : 2 + n_dp], refs[2 + n_dp]
    lat_s, k_s, v_s, q_s, d_s, dk_s, dv_s, dq_s, gl_s, gw_s = refs[3 + n_dp :]
    blocks = in_ref.shape[0]
    seq = lat_s.shape[0]
    scale = WIDTH ** (-0.5)
    per_half = HALF // SUB
    n_x = n_head // 2
    x, core = lax.div(rank_ref[1], 2), lax.rem(rank_ref[1], 2)

    def place(block):
        return pl.multiple_of(order_ref[block] * HALF, HALF)

    for s in range(blocks):
        for half in range(2):
            rows = pl.ds(place(2 * s + half), HALF)
            lo = half * HALF
            q_s[rows, :NOPE] = in_ref[s, lo : lo + HALF, :]
            q_s[rows, NOPE:] = in_ref[s, ROW_ROPE:ROWS_IN, half * ROPE : (half + 1) * ROPE]
            d_s[rows, :] = in_ref[s, ROW_DO + lo : ROW_DO + lo + HALF, :]
    for shift in range(n_head):
        other, back = divmod(shift, n_x)
        p = lax.rem(x + n_x - back, n_x) * 2 + lax.rem(core + other, 2)
        half, i = lax.div(p, per_half), lax.rem(p, per_half)
        for s in range(blocks):
            sub = pl.ds(pl.multiple_of(order_ref[2 * s + half] * HALF + i * SUB, SUB), SUB)
            lat_s[sub, :] = lat_refs[shift][s, :, :LAT]
            k_s[sub, NOPE:] = lat_refs[shift][s, :, LAT:]

    w_both = w_ref[...]
    for t in range(seq // TILE):
        rows = slice(t * TILE, (t + 1) * TILE)
        both = dot_nn(lat_s[rows, :], w_both)
        k_s[rows, :NOPE] = both[:, :NOPE].astype(BF)
        v_s[rows, :] = both[:, NOPE:].astype(BF)

    dk_s[...] = jnp.zeros_like(dk_s)
    dv_s[...] = jnp.zeros_like(dv_s)
    for t in range(seq // TILE):
        rows = slice(t * TILE, (t + 1) * TILE)
        width = (t + 1) * TILE
        q = q_s[rows, :]
        d = d_s[rows, :]
        k = k_s[:width, :]
        scores = dot_nt(k, q) * scale
        key_pos = lax.broadcasted_iota(jnp.int32, (width, TILE), 0)
        row_pos = lax.broadcasted_iota(jnp.int32, (width, TILE), 1) + t * TILE
        masked = jnp.where(key_pos <= row_pos, scores, -jnp.inf)
        top = jnp.max(masked, axis=0, keepdims=True)
        weights = jnp.exp(masked - top)
        probs = weights / jnp.sum(weights, axis=0, keepdims=True)
        probs_b = probs.astype(BF)
        dprob = dot_nt(v_s[:width, :], d)
        drow = jnp.sum(probs_b.astype(F32) * dprob, axis=0, keepdims=True)
        dscore = (probs * (dprob - drow)).astype(BF)
        dq_s[rows, :] = (dot_tn(dscore, k) * scale).astype(BF)
        dk_s[:width, :] += dot_nn(dscore, q)
        dv_s[:width, :] += dot_nn(probs_b, d)

    dk = dk_s[...] * scale
    dkv = jnp.concatenate([dk[:, :NOPE], dv_s[...]], axis=1).astype(BF)
    gw_s[...] = dot_tn(lat_s[...], dkv).astype(BF)
    share = LAT // n_dp
    for shift in range(n_dp):
        target = lax.rem(rank_ref[2] + shift, n_dp)
        gw_refs[shift][...] = gw_s[pl.ds(pl.multiple_of(target * share, share), share), :]
    gl_s[:, :LAT] = dot_nt(dkv, w_both).astype(BF)
    gl_s[:, LAT:] = dk[:, NOPE:].astype(BF)

    for s in range(blocks):
        for half in range(2):
            base = place(2 * s + half)
            rows = pl.ds(base, HALF)
            lo = half * HALF
            gq_ref[s, lo : lo + HALF, :] = dq_s[rows, :NOPE]
            gq_ref[s, ROW_GROPE:ROW_GL, half * ROPE : (half + 1) * ROPE] = dq_s[rows, NOPE:]
    for flip in range(2):
        for shift in range(n_x):
            p = lax.rem(x + shift, n_x) * 2 + lax.rem(core + flip, 2)
            half, i = lax.div(p, per_half), lax.rem(p, per_half)
            for s in range(blocks):
                sub = pl.ds(pl.multiple_of(order_ref[2 * s + half] * HALF + i * SUB, SUB), SUB)
                out_ref = gl_refs[flip].at[shift, s]
                for j in range(LAT // 128):
                    out_ref[SUB * j : SUB * (j + 1), :] = gl_s[sub, 128 * j : 128 * (j + 1)]
                rope = gl_s[sub, LAT:]
                out_ref[SUB * (LAT // 128) :, :] = jnp.concatenate([rope, rope], axis=1)


def fold_kernel(keep_ref, moved_ref, *out_refs):
    for shift, out_ref in enumerate(out_refs):
        out_ref[...] = (keep_ref[shift].astype(F32) + moved_ref[shift].astype(F32)).astype(BF)


def combine_kernel(gq_ref, *refs):
    gl_refs, out_ref = refs[:-1], refs[-1]
    out_ref[:, :ROW_GL, :] = gq_ref[...]
    total = gl_refs[0][...].astype(F32)
    for gl_ref in gl_refs[1:]:
        total = total + gl_ref[...].astype(F32)
    out_ref[:, ROW_GL:, :] = total.astype(BF)


def unpack_kernel(in_ref, gq_ref, gl_ref):
    n = in_ref.shape[0]
    for h in range(n):
        rope = in_ref[h, ROW_GROPE:ROW_GL, :]
        rope = jnp.concatenate([rope[:, :ROPE], rope[:, ROPE:]], axis=0)
        gq_ref[:, h * WIDTH : (h + 1) * WIDTH] = jnp.concatenate([in_ref[h, :NOPE, :], rope], axis=1)
    for j in range(LAT // 128):
        part = in_ref[:, ROW_GL + SUB * j : ROW_GL + SUB * (j + 1), :].astype(F32)
        gl_ref[:, 128 * j : 128 * (j + 1)] = jnp.sum(part, axis=0)
    part = in_ref[:, ROW_GLROPE:ROWS_OUT, :ROPE].astype(F32)
    gl_ref[:, LAT:] = jnp.sum(part, axis=0)


def assemble_kernel(steps, n_dp, rank_ref, *refs):
    n_in = sum(len(group) for group in steps.values())
    in_refs = list(refs[:n_in])
    gk_ref, gv_ref, gk_s, gv_s, sems = refs[-5:]
    share = in_refs[0].shape[1]
    copies = []
    for k, (step, group) in enumerate(steps.items()):
        h = 0
        for in_ref in [in_refs[i] for i in group]:
            for i in range(in_ref.shape[0]):
                part = in_ref[i].astype(F32)
                gk_s[k, :, h * NOPE : (h + 1) * NOPE] = part[:, :NOPE]
                gv_s[k, :, h * VDIM : (h + 1) * VDIM] = part[:, NOPE:]
                h += 1
        source = lax.rem(rank_ref[2] + n_dp - step, n_dp)
        rows = pl.ds(pl.multiple_of(source * share, share), share)
        copies.append(pltpu.make_async_copy(gk_s.at[k], gk_ref.at[rows], sems.at[k, 0]))
        copies.append(pltpu.make_async_copy(gv_s.at[k], gv_ref.at[rows], sems.at[k, 1]))
        copies[-2].start()
        copies[-1].start()
    for copy in copies:
        copy.wait()


def assemble(name, steps, n_dp, ranks, parts, outs, filled=()):
    n, rows = len(steps), parts[0].shape[1]
    return call(
        functools.partial(assemble_kernel, steps, n_dp),
        name,
        (ranks,),
        (*parts, *filled),
        outs,
        scratch=[pltpu.VMEM((n, rows, outs[i].shape[1]), F32) for i in range(2)]
        + [pltpu.SemaphoreType.DMA((n, 2))],
        in_specs=[whole(part.shape) for part in parts] + [ANY] * len(filled),
        out_specs=[ANY, ANY],
        aliases={1 + len(parts) + i: i for i in range(len(filled))},
    )


def shifted(x, axis, n, shift):
    return lax.ppermute(x, axis, [(i, (i + shift) % n) for i in range(n)])


def whole(shape):
    return pl.BlockSpec(shape, lambda i, *scalars: (0,) * len(shape))


def call(
    kernel, name, scalars, inputs, outs, scratch=(), in_specs=None, flops=0, vmem=16,
    out_specs=None, aliases=None,
):
    moved = sum(x.size * x.dtype.itemsize for x in inputs) + sum(
        x.size * x.dtype.itemsize for x in outs
    )
    return pl.pallas_call(
        kernel,
        grid_spec=pltpu.PrefetchScalarGridSpec(
            num_scalar_prefetch=len(scalars),
            grid=(1,),
            in_specs=in_specs or [whole(x.shape) for x in inputs],
            out_specs=out_specs or [whole(x.shape) for x in outs],
            scratch_shapes=list(scratch),
        ),
        out_shape=list(outs),
        input_output_aliases=aliases or {},
        compiler_params=pltpu.CompilerParams(vmem_limit_bytes=vmem * 1024 * 1024),
        cost_estimate=pl.CostEstimate(flops=flops, bytes_accessed=moved, transcendentals=0),
        name=name,
    )(*scalars, *inputs)


def on_device(n_dp, n_ctx, n_head, query, latent, w_uk, w_uv, grad_out, block_order):
    seq = n_ctx * n_head * SUB
    rows = query.shape[1]
    shape = jax.ShapeDtypeStruct
    ranks = jnp.stack([lax.axis_index(a).astype(jnp.int32) for a in ("ctx", "head", "dp")])

    lat_mine = lax.all_to_all(
        jnp.broadcast_to(latent, (n_ctx, SUB, LAT + ROPE)), "ctx", 0, 0, tiled=True
    )
    flip = [(i, i ^ 1) for i in range(n_head)]
    lat_all = [lat_mine] + [shifted(lat_mine, "head", n_head, 2 * i) for i in range(1, n_head // 2)]
    lat_all += [lax.ppermute(part, "head", flip) for part in lat_all]
    head_cols = pl.BlockSpec((LAT, NOPE), lambda i, rank: (0, rank[0]))
    packed, w_both = call(
        pack_kernel,
        "pack",
        (ranks,),
        (query[0], grad_out[0], w_uk, w_uv),
        [shape((n_ctx, ROWS_IN, 128), BF), shape((LAT, NOPE + VDIM), BF)],
        in_specs=[whole(query.shape[1:]), whole(grad_out.shape[1:]), head_cols, head_cols],
    )
    mine = lax.all_to_all(packed, "ctx", 0, 0, tiled=True)

    gl_keep, gl_send, *gw_parts, gq_part = call(
        functools.partial(attention_kernel, n_head, n_dp),
        "attention_backward",
        (block_order, ranks),
        (mine, w_both, *lat_all),
        [shape((n_head // 2, n_ctx, SUB * (LAT // 128) + SUB, 128), BF)] * 2
        + [shape((LAT // n_dp, NOPE + VDIM), BF)] * n_dp
        + [shape((n_ctx, ROW_GL, 128), BF)],
        scratch=[
            pltpu.VMEM((seq, LAT), BF),
            pltpu.VMEM((seq, WIDTH), BF),
            pltpu.VMEM((seq, VDIM), BF),
            pltpu.VMEM((seq, WIDTH), BF),
            pltpu.VMEM((seq, VDIM), BF),
            pltpu.VMEM((seq, WIDTH), F32),
            pltpu.VMEM((seq, VDIM), F32),
            pltpu.VMEM((seq, WIDTH), BF),
            pltpu.VMEM((seq, LAT + ROPE), BF),
            pltpu.VMEM((LAT, NOPE + VDIM), BF),
        ],
        flops=3 * 10**9,
        vmem=28,
    )

    gw_sum = gw_parts[0].astype(F32)
    for i in range(1, n_dp):
        gw_sum = gw_sum + shifted(gw_parts[i], "dp", n_dp, i).astype(F32)
    gw_sum = gw_sum.astype(BF)
    gl_recv = lax.ppermute(gl_send, "head", flip)
    gw_sum, gl_recv = lax.optimization_barrier((gw_sum, gl_recv))
    folded = call(
        fold_kernel,
        "fold",
        (),
        (gl_keep, gl_recv),
        [shape(gl_keep.shape[1:], BF)] * (n_head // 2),
    )
    gw_ctx = lax.all_to_all(
        jnp.broadcast_to(gw_sum[None], (n_ctx,) + gw_sum.shape), "ctx", 0, 0, tiled=True
    )
    gl_moved = [folded[0]] + [
        lax.ppermute(folded[i], "head", [(j, (j + 2 * i) % n_head) for j in range(n_head)])
        for i in range(1, n_head // 2)
    ]
    half = n_ctx // 2
    before, after = shifted(gw_ctx, "dp", n_dp, 1), shifted(gw_ctx, "dp", n_dp, n_dp - 1)
    opposite = [
        shifted(before[:half], "dp", n_dp, 1),
        shifted(after[half:], "dp", n_dp, n_dp - 1),
    ]
    back = call(
        combine_kernel,
        "combine",
        (),
        (gq_part, *gl_moved),
        [shape((n_ctx, ROWS_OUT, 128), BF)],
    )[0]
    back = lax.all_to_all(back, "ctx", 0, 0, tiled=True)
    grad_query, grad_latent = call(
        unpack_kernel,
        "unpack",
        (),
        (back,),
        [shape((rows, n_ctx * WIDTH), BF), shape((SUB, LAT + ROPE), F32)],
    )
    outs = [shape((LAT, n_ctx * NOPE), F32), shape((LAT, n_ctx * VDIM), F32)]
    filled = assemble(
        "assemble_near", {0: [0], 1: [1], 3: [2]}, n_dp, ranks, [gw_ctx, before, after], outs
    )
    grad_query, grad_latent, *opposite = lax.optimization_barrier(
        (grad_query, grad_latent, *opposite)
    )
    grad_w_uk, grad_w_uv = assemble(
        "assemble_far", {2: [0, 1]}, n_dp, ranks, opposite, outs, filled
    )
    return (grad_query[None], grad_latent[None], grad_w_uk, grad_w_uv)


def solution(mesh):
    sizes = mesh.shape
    return jax.shard_map(
        functools.partial(on_device, sizes["dp"], sizes["ctx"], sizes["head"]),
        mesh=mesh,
        in_specs=(
            P("dp", "ctx", "head"),
            P("dp", ("ctx", "head"), None),
            P(None, "head"),
            P(None, "head"),
            P("dp", "ctx", "head"),
            P(),
        ),
        out_specs=(
            P("dp", "ctx", "head"),
            P("dp", ("ctx", "head"), None),
            P(None, "head"),
            P(None, "head"),
        ),
        check_vma=False,
    )
```
